32 devices in a mesh: row: 8 (over y, x, core), col: 4 (over z).
Axes of the slice: x: 2, y: 2, z: 4, core: 2. Of those that a mesh axis runs over, the one named last changes fastest.
Arguments:
- similarity: float32 [2048, 2048], P('row', 'col'), may hold values from 0.1 to 500
- pattern: int32 [8, 8], P('row', 'col'), may hold values from 0 to 1, as said below
Outputs:
- clustered: float32 [2048, 2048], P('row', 'col')
The draws below stay inside these ranges and needn't reach their ends.
Inputs may be any that keep to these rules, and one draw needn't show every extreme that they name: `pattern`: every diagonal tile (g, g) is stored.
All inputs are finite; a program needn't handle non-finite values.
Results may differ from the reference program's by a relative error of at most 0.0003.
Values may be sent and summed in bfloat16 or wider, within the bound.
No kernel may reach another device: no remote copies, remote signals or barrier semaphores. Data moves between devices by JAX's collectives and lax.ppermute only.
A program may use at most 64 MiB of HBM per device.

```python
import math
import jax
import jax.numpy as jnp
from jax import lax

TILE = 256
ITERS = 1
NT = 8
NV = 2048


def draw_similarity(key, part):
    first = jax.random.fold_in(key, 11)
    second = jax.random.fold_in(key, 12)
    third = jax.random.fold_in(key, 13)
    place = jnp.arange(NV).astype(jnp.float32) / NV
    base = jax.random.uniform(first, (NV, NV), jnp.float32, 0.5, 1.5)
    row_scale = jnp.exp(math.log(3.0) * place) * jnp.exp(jax.random.uniform(second, (NV,), jnp.float32, 0.0, math.log(10.0)))
    col_scale = jnp.exp(jax.random.uniform(third, (NV,), jnp.float32, 0.0, math.log(10.0)))
    return base * row_scale[:, None] * col_scale[None, :]


def draw_pattern(key, part):
    picks = jax.random.randint(jax.random.fold_in(key, 21), (NT, NT), 0, 8)
    stored = (picks < 3).astype(jnp.int32)
    index = jnp.arange(NT)
    diagonal = (index[:, None] == index[None, :]).astype(jnp.int32)
    return jnp.maximum(stored, diagonal)


def setup_inputs(seed: int = 0) -> dict:
    key_list = jax.random.split(jax.random.key(seed), 3)
    similarity = draw_similarity(jax.random.fold_in(key_list[2], 71), 0)
    pattern = draw_pattern(jax.random.fold_in(key_list[2], 71), 0)
    return {"similarity": similarity, "pattern": pattern}


def spread(pattern):
    rows, cols = pattern.shape
    values = pattern.astype(jnp.float32)
    return jnp.broadcast_to(values[:, None, :, None], (rows, TILE, cols, TILE)).reshape(rows * TILE, cols * TILE)


def reference(similarity, pattern):
    cells = spread(pattern)
    held = similarity * cells
    matrix = held * (NV / jnp.sum(held, axis=0))[None, :]
    for step in range(ITERS):
        operand = lax.optimization_barrier(matrix.astype(jnp.bfloat16)).astype(jnp.float32)
        expanded = jnp.dot(operand, operand, precision=lax.Precision.HIGHEST, preferred_element_type=jnp.float32) * cells
        inflated = expanded * expanded
        matrix = inflated * (NV / jnp.sum(inflated, axis=0))[None, :]
    return matrix
```

```python
import jax
import jax.numpy as jnp
from jax import lax
from jax.sharding import PartitionSpec as P

TILE = 256


def spread(pattern):
    rows, cols = pattern.shape
    values = pattern.astype(jnp.float32)
    return jnp.broadcast_to(values[:, None, :, None], (rows, TILE, cols, TILE)).reshape(
        rows * TILE, cols * TILE
    )


def swap(x, axis, mask):
    size = lax.axis_size(axis)
    return lax.ppermute(x, axis, [(i, i ^ mask) for i in range(size)])


def total(x, axis):
    mask = 1
    while mask < lax.axis_size(axis):
        x = x + swap(x, axis, mask)
        mask *= 2
    return x


def gather_rows(x):
    size, me = lax.axis_size("row"), lax.axis_index("row")
    depth = x.shape[0]
    got = {0: x}
    for mask in sorted(range(2, size, 2), reverse=True):
        got[mask] = swap(x, "row", mask)
    for mask in range(0, size, 2):
        got[mask + 1] = swap(got[mask], "row", 1)
    whole = jnp.zeros((size * depth, x.shape[1]), x.dtype)
    for mask in range(size):
        whole = lax.dynamic_update_slice(whole, got[mask], ((me ^ mask) * depth, 0))
    return whole


def gather_columns(x):
    size, me = lax.axis_size("col"), lax.axis_index("col")
    width = x.shape[1]
    whole = jnp.zeros((x.shape[0], size * width), x.dtype)
    got = {0: x}
    for mask in range(1, size):
        got[mask] = swap(x, "col", mask)
    for mask in range(size):
        whole = lax.dynamic_update_slice(whole, got[mask], (0, (me ^ mask) * width))
    return whole


def product(operand):
    left = gather_columns(operand)
    right = gather_rows(operand)
    return jnp.dot(left, right, preferred_element_type=jnp.float32)


def shards(similarity, pattern):
    cells = spread(pattern)
    total_rows = similarity.shape[0] * lax.axis_size("row")
    held = similarity * cells
    start_total = total(jnp.sum(held, axis=0), "row")
    matrix = held * (total_rows / start_total)[None, :]
    operand = matrix.astype(jnp.bfloat16)
    expanded = product(operand) * cells
    inflated = expanded * expanded
    sums = total(jnp.sum(inflated, axis=0), "row")
    return inflated * (total_rows / sums)[None, :]


def solution(mesh):
    placed = (P("row", "col"), P("row", "col"))
    return jax.shard_map(
        shards, mesh=mesh, in_specs=placed, out_specs=P("row", "col"), check_vma=False
    )
```

```python
import jax
import jax.numpy as jnp
from jax import lax
from jax.sharding import PartitionSpec as P

TILE = 256


def spread(pattern):
    rows, cols = pattern.shape
    values = pattern.astype(jnp.float32)
    return jnp.broadcast_to(values[:, None, :, None], (rows, TILE, cols, TILE)).reshape(
        rows * TILE, cols * TILE
    )


def swap(x, axis, mask):
    size = lax.axis_size(axis)
    return lax.ppermute(x, axis, [(i, i ^ mask) for i in range(size)])


def total(x, axis):
    mask = 1
    while mask < lax.axis_size(axis):
        x = x + swap(x, axis, mask)
        mask *= 2
    return x


def join_rows(blocks):
    size, me = lax.axis_size("row"), lax.axis_index("row")
    depth, width = blocks[0].shape
    whole = jnp.zeros((size * depth, width), blocks[0].dtype)
    for mask in range(size):
        whole = lax.dynamic_update_slice(whole, blocks[mask], ((me ^ mask) * depth, 0))
    return whole


def join_columns(blocks):
    size, me = lax.axis_size("col"), lax.axis_index("col")
    depth, width = blocks[0].shape
    whole = jnp.zeros((depth, size * width), blocks[0].dtype)
    for mask in range(size):
        whole = lax.dynamic_update_slice(whole, blocks[mask], (0, (me ^ mask) * width))
    return whole


def scaled(held, scale):
    return (held * scale[None, :]).astype(jnp.bfloat16)


def gather_columns(x):
    got = {0: x}
    for mask in range(1, lax.axis_size("col")):
        low = mask & -mask
        got[mask] = swap(got[mask - low], "col", low)
    return join_columns(got)


def gather_rows(x):
    got = {0: x}
    for mask in range(2, lax.axis_size("row"), 2):
        got[mask] = swap(x, "row", mask)
    for mask in range(0, lax.axis_size("row"), 2):
        got[mask + 1] = swap(got[mask], "row", 1)
    return join_rows(got)


def shards(similarity, pattern):
    cells = spread(pattern)
    total_rows = similarity.shape[0] * lax.axis_size("row")
    held = similarity * cells
    scale = total_rows / total(jnp.sum(held, axis=0), "row")
    operand = scaled(held, scale)

    left, right = gather_columns(operand), gather_rows(operand)
    expanded = jnp.dot(left, right, preferred_element_type=jnp.float32) * cells
    inflated = expanded * expanded
    sums = total(jnp.sum(inflated, axis=0), "row")
    return inflated * (total_rows / sums)[None, :]


def solution(mesh):
    placed = (P("row", "col"), P("row", "col"))
    return jax.shard_map(
        shards, mesh=mesh, in_specs=placed, out_specs=P("row", "col"), check_vma=False
    )
```

```python
import jax
import jax.numpy as jnp
from jax import lax
from jax.sharding import PartitionSpec as P

TILE = 256


def spread(pattern):
    rows, cols = pattern.shape
    values = pattern.astype(jnp.float32)
    return jnp.broadcast_to(values[:, None, :, None], (rows, TILE, cols, TILE)).reshape(
        rows * TILE, cols * TILE
    )


def swap(x, axis, mask):
    size = lax.axis_size(axis)
    return lax.ppermute(x, axis, [(i, i ^ mask) for i in range(size)])


def total(x, axis):
    mask = 1
    while mask < lax.axis_size(axis):
        x = x + swap(x, axis, mask)
        mask *= 2
    return x


def join_rows(blocks):
    size, me = lax.axis_size("row"), lax.axis_index("row")
    depth, width = blocks[0].shape
    whole = jnp.zeros((size * depth, width), blocks[0].dtype)
    for mask in range(size):
        whole = lax.dynamic_update_slice(whole, blocks[mask], ((me ^ mask) * depth, 0))
    return whole


def join_columns(blocks):
    size, me = lax.axis_size("col"), lax.axis_index("col")
    depth, width = blocks[0].shape
    whole = jnp.zeros((depth, size * width), blocks[0].dtype)
    for mask in range(size):
        whole = lax.dynamic_update_slice(whole, blocks[mask], (0, (me ^ mask) * width))
    return whole


def scaled(held, scale):
    return (held * scale[None, :]).astype(jnp.bfloat16)


def gather_columns(x):
    got = {0: x}
    for mask in range(1, lax.axis_size("col")):
        low = mask & -mask
        got[mask] = swap(got[mask - low], "col", low)
    return join_columns(got)


def gather_rows(x):
    got = {0: x}
    for mask in range(2, lax.axis_size("row"), 2):
        got[mask] = swap(x, "row", mask)
    for mask in range(0, lax.axis_size("row"), 2):
        got[mask + 1] = swap(got[mask], "row", 1)
    return join_rows(got)


def after(x, other):
    return lax.optimization_barrier((x, other))[0]


def gather(x):
    first = x.shape[0] * 5 // 8 // 16 * 16
    far = [swap(x[:first], "col", 2), swap(x[first:], "col", 2)]
    rows = {0: x, 2: swap(x, "row", 2), 4: swap(x, "row", 4)}
    rows[6] = swap(after(x, far[0]), "row", 6)
    near = swap(x, "col", 1)
    rows[1] = swap(after(x, near), "row", 1)
    passed = [swap(after(far[0], rows[2]), "col", 1), swap(far[1], "col", 1)]
    for mask in (2, 4, 6):
        rows[mask + 1] = swap(rows[mask], "row", 1)
    columns = [x, near, jnp.concatenate(far), jnp.concatenate(passed)]
    return join_columns(columns), join_rows(rows)


def shards(similarity, pattern):
    cells = spread(pattern)
    total_rows = similarity.shape[0] * lax.axis_size("row")
    held = similarity * cells
    scale = total_rows / total(jnp.sum(held, axis=0), "row")
    operand = scaled(held, scale)
    if (lax.axis_size("row"), lax.axis_size("col")) == (8, 4):
        left, right = gather(operand)
    else:
        left, right = gather_columns(operand), gather_rows(operand)
    expanded = jnp.dot(left, right, preferred_element_type=jnp.float32) * cells
    inflated = expanded * expanded
    sums = total(jnp.sum(inflated, axis=0), "row")
    return inflated * (total_rows / sums)[None, :]


def solution(mesh):
    placed = (P("row", "col"), P("row", "col"))
    return jax.shard_map(
        shards, mesh=mesh, in_specs=placed, out_specs=P("row", "col"), check_vma=False
    )
```

```python
import jax
import jax.numpy as jnp
from jax import lax
from jax.sharding import PartitionSpec as P

TILE = 256


def spread(pattern):
    rows, cols = pattern.shape
    values = pattern.astype(jnp.float32)
    return jnp.broadcast_to(values[:, None, :, None], (rows, TILE, cols, TILE)).reshape(
        rows * TILE, cols * TILE
    )


def swap(x, axis, mask):
    size = lax.axis_size(axis)
    return lax.ppermute(x, axis, [(i, i ^ mask) for i in range(size)])


def total(x, axis):
    mask = 1
    while mask < lax.axis_size(axis):
        x = x + swap(x, axis, mask)
        mask *= 2
    return x


def join_rows(blocks):
    size, me = lax.axis_size("row"), lax.axis_index("row")
    depth, width = blocks[0].shape
    whole = jnp.zeros((size * depth, width), blocks[0].dtype)
    for mask in range(size):
        whole = lax.dynamic_update_slice(whole, blocks[mask], ((me ^ mask) * depth, 0))
    return whole


def join_columns(blocks):
    size, me = lax.axis_size("col"), lax.axis_index("col")
    depth, width = blocks[0].shape
    whole = jnp.zeros((depth, size * width), blocks[0].dtype)
    for mask in range(size):
        whole = lax.dynamic_update_slice(whole, blocks[mask], (0, (me ^ mask) * width))
    return whole


def scaled(held, scale):
    return (held * scale[None, :]).astype(jnp.bfloat16)


def gather_columns(x):
    got = {0: x}
    for mask in range(1, lax.axis_size("col")):
        low = mask & -mask
        got[mask] = swap(got[mask - low], "col", low)
    return join_columns(got)


def gather_rows(x):
    got = {0: x}
    for mask in range(2, lax.axis_size("row"), 2):
        got[mask] = swap(x, "row", mask)
    for mask in range(0, lax.axis_size("row"), 2):
        got[mask + 1] = swap(got[mask], "row", 1)
    return join_rows(got)


def after(x, other):
    return lax.optimization_barrier((x, other))[0]


def gather(x):
    first = x.shape[0] * 5 // 8 // 16 * 16
    rows = {0: x}
    for mask in (2, 4, 6):
        rows[mask] = swap(x, "row", mask)
    near = swap(x, "col", 1)
    rows[1] = swap(after(x, near), "row", 1)
    far = [swap(x[:first], "col", 2)]
    passed = [swap(far[0], "col", 1)]
    far.append(swap(after(x, far[0])[first:], "col", 2))
    passed.append(swap(after(far[1], rows[2]), "col", 1))
    for mask in (2, 4, 6):
        rows[mask + 1] = swap(rows[mask], "row", 1)
    columns = [x, near, jnp.concatenate(far), jnp.concatenate(passed)]
    return join_columns(columns), join_rows(rows)


def shards(similarity, pattern):
    cells = spread(pattern)
    total_rows = similarity.shape[0] * lax.axis_size("row")
    held = similarity * cells
    scale = total_rows / total(jnp.sum(held, axis=0), "row")
    operand = scaled(held, scale)
    if (lax.axis_size("row"), lax.axis_size("col")) == (8, 4):
        left, right = gather(operand)
    else:
        left, right = gather_columns(operand), gather_rows(operand)
    expanded = jnp.dot(left, right, preferred_element_type=jnp.float32) * cells
    inflated = expanded * expanded
    sums = total(jnp.sum(inflated, axis=0), "row")
    return inflated * (total_rows / sums)[None, :]


def solution(mesh):
    placed = (P("row", "col"), P("row", "col"))
    return jax.shard_map(
        shards, mesh=mesh, in_specs=placed, out_specs=P("row", "col"), check_vma=False
    )
```

```python
import jax
import jax.numpy as jnp
from jax import lax
from jax.sharding import PartitionSpec as P

TILE = 256


def spread(pattern):
    rows, cols = pattern.shape
    values = pattern.astype(jnp.float32)
    return jnp.broadcast_to(values[:, None, :, None], (rows, TILE, cols, TILE)).reshape(
        rows * TILE, cols * TILE
    )


def swap(x, axis, mask):
    size = lax.axis_size(axis)
    return lax.ppermute(x, axis, [(i, i ^ mask) for i in range(size)])


def total(x, axis):
    mask = 1
    while mask < lax.axis_size(axis):
        x = x + swap(x, axis, mask)
        mask *= 2
    return x


def join_rows(blocks):
    size, me = lax.axis_size("row"), lax.axis_index("row")
    depth, width = blocks[0].shape
    whole = jnp.zeros((size * depth, width), blocks[0].dtype)
    for mask in range(size):
        whole = lax.dynamic_update_slice(whole, blocks[mask], ((me ^ mask) * depth, 0))
    return whole


def join_columns(blocks):
    size, me = lax.axis_size("col"), lax.axis_index("col")
    depth, width = blocks[0].shape
    whole = jnp.zeros((depth, size * width), blocks[0].dtype)
    for mask in range(size):
        whole = lax.dynamic_update_slice(whole, blocks[mask], (0, (me ^ mask) * width))
    return whole


def scaled(held, scale):
    return (held * scale[None, :]).astype(jnp.bfloat16)


def gather_columns(x):
    got = {0: x}
    for mask in range(1, lax.axis_size("col")):
        low = mask & -mask
        got[mask] = swap(got[mask - low], "col", low)
    return join_columns(got)


def gather_rows(x):
    got = {0: x}
    for mask in range(2, lax.axis_size("row"), 2):
        got[mask] = swap(x, "row", mask)
    for mask in range(0, lax.axis_size("row"), 2):
        got[mask + 1] = swap(got[mask], "row", 1)
    return join_rows(got)


def after(x, other):
    return lax.optimization_barrier((x, other))[0]


def gather(x):
    first = x.shape[0] * 9 // 16 // 16 * 16
    rows = {0: x}
    for mask in (2, 4, 6):
        rows[mask] = swap(x, "row", mask)
    near = swap(x, "col", 1)
    rows[1] = swap(after(x, near), "row", 1)
    far = [swap(x[:first], "col", 2)]
    passed = [swap(far[0], "col", 1)]
    far.append(swap(after(x, far[0])[first:], "col", 2))
    passed.append(swap(after(far[1], rows[2]), "col", 1))
    for mask in (2, 4, 6):
        rows[mask + 1] = swap(rows[mask], "row", 1)
    columns = [x, near, jnp.concatenate(far), jnp.concatenate(passed)]
    return join_columns(columns), join_rows(rows)


def shards(similarity, pattern):
    cells = spread(pattern)
    total_rows = similarity.shape[0] * lax.axis_size("row")
    held = similarity * cells
    scale = total_rows / total(jnp.sum(held, axis=0), "row")
    operand = scaled(held, scale)
    if (lax.axis_size("row"), lax.axis_size("col")) == (8, 4):
        left, right = gather(operand)
    else:
        left, right = gather_columns(operand), gather_rows(operand)
    expanded = jnp.dot(left, right, preferred_element_type=jnp.float32) * cells
    inflated = expanded * expanded
    sums = total(jnp.sum(inflated, axis=0), "row")
    return inflated * (total_rows / sums)[None, :]


def solution(mesh):
    placed = (P("row", "col"), P("row", "col"))
    return jax.shard_map(
        shards, mesh=mesh, in_specs=placed, out_specs=P("row", "col"), check_vma=False
    )
```

```python
import jax
import jax.numpy as jnp
from jax import lax
from jax.sharding import PartitionSpec as P

TILE = 256


def spread(pattern):
    rows, cols = pattern.shape
    values = pattern.astype(jnp.float32)
    return jnp.broadcast_to(values[:, None, :, None], (rows, TILE, cols, TILE)).reshape(
        rows * TILE, cols * TILE
    )


def swap(x, axis, mask):
    size = lax.axis_size(axis)
    return lax.ppermute(x, axis, [(i, i ^ mask) for i in range(size)])


def total(x, axis):
    mask = 1
    while mask < lax.axis_size(axis):
        x = x + swap(x, axis, mask)
        mask *= 2
    return x


def join_rows(blocks):
    size, me = lax.axis_size("row"), lax.axis_index("row")
    depth, width = blocks[0].shape
    whole = jnp.zeros((size * depth, width), blocks[0].dtype)
    for mask in range(size):
        whole = lax.dynamic_update_slice(whole, blocks[mask], ((me ^ mask) * depth, 0))
    return whole


def join_columns(blocks, zero=0):
    size, me = lax.axis_size("col"), lax.axis_index("col")
    depth, width = blocks[0].shape
    whole = jnp.full((depth, size * width), zero, blocks[0].dtype)
    for mask in range(size):
        whole = lax.dynamic_update_slice(whole, blocks[mask], (0, (me ^ mask) * width))
    return whole


def scaled(held, scale):
    return (held * scale[None, :]).astype(jnp.bfloat16)


def gather_columns(x):
    got = {0: x}
    for mask in range(1, lax.axis_size("col")):
        low = mask & -mask
        got[mask] = swap(got[mask - low], "col", low)
    return join_columns(got)


def gather_rows(x):
    got = {0: x}
    for mask in range(2, lax.axis_size("row"), 2):
        got[mask] = swap(x, "row", mask)
    for mask in range(0, lax.axis_size("row"), 2):
        got[mask + 1] = swap(got[mask], "row", 1)
    return join_rows(got)


def after(x, other):
    return lax.optimization_barrier((x, other))[0]


def gather(x):
    first = x.shape[0] * 5 // 8 // 16 * 16
    rows = {0: x}
    for mask in (2, 4, 6):
        rows[mask] = swap(x, "row", mask)
    near = swap(x, "col", 1)
    rows[1] = swap(after(x, near), "row", 1)
    far = [swap(x[:first], "col", 2)]
    passed = [swap(far[0], "col", 1)]
    far.append(swap(after(x, far[0])[first:], "col", 2))
    passed.append(swap(after(far[1], rows[2]), "col", 1))
    for mask in (2, 4, 6):
        rows[mask + 1] = swap(rows[mask], "row", 1)
    columns = [x, near, jnp.concatenate(far), jnp.concatenate(passed)]
    zero = after(jnp.zeros((), x.dtype), far[0])
    return join_columns(columns, zero), join_rows(rows)


def shards(similarity, pattern):
    cells = spread(pattern)
    total_rows = similarity.shape[0] * lax.axis_size("row")
    held = similarity * cells
    scale = total_rows / total(jnp.sum(held, axis=0), "row")
    operand = scaled(held, scale)
    if (lax.axis_size("row"), lax.axis_size("col")) == (8, 4):
        left, right = gather(operand)
    else:
        left, right = gather_columns(operand), gather_rows(operand)
    expanded = jnp.dot(left, right, preferred_element_type=jnp.float32) * cells
    inflated = expanded * expanded
    sums = total(jnp.sum(inflated, axis=0), "row")
    return inflated * (total_rows / sums)[None, :]


def solution(mesh):
    placed = (P("row", "col"), P("row", "col"))
    return jax.shard_map(
        shards, mesh=mesh, in_specs=placed, out_specs=P("row", "col"), check_vma=False
    )
```

```python
import jax
import jax.numpy as jnp
from jax import lax
from jax.sharding import PartitionSpec as P

TILE = 256


def spread(pattern):
    rows, cols = pattern.shape
    values = pattern.astype(jnp.float32)
    return jnp.broadcast_to(values[:, None, :, None], (rows, TILE, cols, TILE)).reshape(
        rows * TILE, cols * TILE
    )


def swap(x, axis, mask):
    size = lax.axis_size(axis)
    return lax.ppermute(x, axis, [(i, i ^ mask) for i in range(size)])


def total(x, axis):
    mask = 1
    while mask < lax.axis_size(axis):
        x = x + swap(x, axis, mask)
        mask *= 2
    return x


def join_rows(blocks):
    size, me = lax.axis_size("row"), lax.axis_index("row")
    depth, width = blocks[0].shape
    whole = jnp.zeros((size * depth, width), blocks[0].dtype)
    for mask in range(size):
        whole = lax.dynamic_update_slice(whole, blocks[mask], ((me ^ mask) * depth, 0))
    return whole


def join_columns(blocks):
    size, me = lax.axis_size("col"), lax.axis_index("col")
    depth, width = blocks[0].shape
    whole = jnp.zeros((depth, size * width), blocks[0].dtype)
    for mask in range(size):
        whole = lax.dynamic_update_slice(whole, blocks[mask], (0, (me ^ mask) * width))
    return whole


def scaled(held, scale):
    return (held * scale[None, :]).astype(jnp.bfloat16)


def gather_columns(x):
    got = {0: x}
    for mask in range(1, lax.axis_size("col")):
        low = mask & -mask
        got[mask] = swap(got[mask - low], "col", low)
    return join_columns(got)


def gather_rows(x):
    got = {0: x}
    for mask in range(2, lax.axis_size("row"), 2):
        got[mask] = swap(x, "row", mask)
    for mask in range(0, lax.axis_size("row"), 2):
        got[mask + 1] = swap(got[mask], "row", 1)
    return join_rows(got)


def after(x, other):
    return lax.optimization_barrier((x, other))[0]


def gather(x):
    first = x.shape[0] * 9 // 16 // 16 * 16
    rows = {0: x}
    for mask in (2, 4, 6):
        rows[mask] = swap(x, "row", mask)
    near = swap(x, "col", 1)
    rows[1] = swap(after(x, near), "row", 1)
    far = [swap(x[:first], "col", 2)]
    passed = [swap(far[0], "col", 1)]
    far.append(swap(after(x, far[0])[first:], "col", 2))
    passed.append(swap(after(far[1], rows[2]), "col", 1))
    rows[3] = swap(after(rows[2], far[1]), "row", 1)
    for mask in (4, 6):
        rows[mask + 1] = swap(rows[mask], "row", 1)
    columns = [x, near, jnp.concatenate(far), jnp.concatenate(passed)]
    return join_columns(columns), join_rows(rows)


def shards(similarity, pattern):
    cells = spread(pattern)
    total_rows = similarity.shape[0] * lax.axis_size("row")
    held = similarity * cells
    scale = total_rows / total(jnp.sum(held, axis=0), "row")
    operand = scaled(held, scale)
    if (lax.axis_size("row"), lax.axis_size("col")) == (8, 4):
        left, right = gather(operand)
    else:
        left, right = gather_columns(operand), gather_rows(operand)
    expanded = jnp.dot(left, right, preferred_element_type=jnp.float32) * cells
    inflated = expanded * expanded
    sums = total(jnp.sum(inflated, axis=0), "row")
    return inflated * (total_rows / sums)[None, :]


def solution(mesh):
    placed = (P("row", "col"), P("row", "col"))
    return jax.shard_map(
        shards, mesh=mesh, in_specs=placed, out_specs=P("row", "col"), check_vma=False
    )
```
